128 devices in a mesh: ctx: 8 (over x, z_lo), head: 16 (over z_hi, y, core).
Axes of the slice: x: 4, y: 4, z: 4 (z_hi: 2, z_lo: 2; z = z_hi * 2 + z_lo), core: 2. Of those that a mesh axis runs over, the one named last changes fastest.
Arguments:
- queries: bfloat16 [4096, 24576], P('ctx', 'head'), may hold values from -300 to 300
- latents: bfloat16 [4096, 576], P('ctx'), may hold values from -1000 to 1000
- block_order: int32 [16], replicated, may hold values from 0 to 15, each once
- norm_gain: float32 [512], replicated, may hold values from 0.1 to 1.9
- w_kv_up: bfloat16 [512, 32768], P(None, 'head'), may hold values from -0.25 to 0.25
- w_out: bfloat16 [16384, 7168], P('head', 'ctx'), may hold values from -0.046875 to 0.046875
Outputs:
- mixed: bfloat16 [4096, 7168], P(('ctx', 'head'))
The draws below stay inside these ranges and needn't reach their ends.
Inputs may be any that keep to these rules, and one draw needn't show every extreme that they name: `block_order`: each block of 0 to 2 * 8 - 1 stands in exactly one slot.
All inputs are finite; a program needn't handle non-finite values.
Results may differ from the reference program's by a relative error of at most 0.02.
Values may be sent and summed in bfloat16 or wider, within the bound.
No kernel may reach another device: no remote copies, remote signals or barrier semaphores. Data moves between devices by JAX's collectives and lax.ppermute only.
A program may use at most 320 MiB of HBM per device.

```python
import math
import jax
import jax.numpy as jnp
from jax import lax

D = 7168
KV_RANK = 512
ROPE = 64
PLAIN_PART_SIZE = 128
VHEAD = 128
BLOCK = 256
HEADS = 128
TOKENS = 4096
N_CTX = 8


def rope_base(key):
    return jnp.clip(jax.random.normal(key, (TOKENS, ROPE), jnp.float32), -4.0, 4.0)


def draw_latents(key, part):
    rotary_part = rope_base(key)
    key = jax.random.fold_in(key, 3)
    first_key, second_key, third_key = jax.random.split(key, 3)
    frequency_base = jnp.clip(jax.random.normal(first_key, (TOKENS, KV_RANK), jnp.float32), -4.0, 4.0)
    row_scale = jnp.exp(jax.random.uniform(second_key, (TOKENS, 1), jnp.float32, 0.0, math.log(10.0)))
    col_scale = jnp.exp(jax.random.uniform(third_key, (1, KV_RANK), jnp.float32, 0.0, math.log(10.0)))
    return jnp.concatenate([frequency_base * row_scale * col_scale, rotary_part], axis=1).astype(jnp.bfloat16)


def draw_queries(key, part):
    key = jax.random.fold_in(key, 5)
    frequency_base = jnp.clip(jax.random.normal(key, (TOKENS, HEADS, PLAIN_PART_SIZE + ROPE), jnp.float32), -4.0, 4.0)
    return frequency_base.reshape(TOKENS, HEADS * (PLAIN_PART_SIZE + ROPE)).astype(jnp.bfloat16)


def level_of(key, extent, shards, low, high):
    def one(axis_at, shards_of):
        draws = jax.random.uniform(jax.random.fold_in(jax.random.fold_in(key, 6), axis_at), (shards_of,), jnp.float32, low / len(shards), high / len(shards))
        return jnp.repeat(jnp.exp(draws), extent[axis_at] // shards_of).reshape((-1,) + (1,) * (len(extent) - axis_at - 1))

    level = one(*shards[0])
    for cut in shards[1:]:
        level = level * one(*cut)
    return level


def normal_values(rng, extent, deviation, limit, shards=(), kind=jnp.bfloat16):
    result = deviation * jax.random.normal(rng, extent, jnp.float32)
    if shards:
        result = result * level_of(rng, extent, shards, -0.22, 0.18)
    return jnp.clip(result, -limit, limit).astype(kind)


def setup_inputs(seed: int = 0) -> dict:
    key_list = jax.random.split(jax.random.key(seed), 7)
    return {
        "queries": draw_queries(jax.random.fold_in(key_list[6], 71), 0),
        "latents": draw_latents(jax.random.fold_in(key_list[6], 71), 0),
        "block_order": jax.random.permutation(key_list[2], 2 * N_CTX).astype(jnp.int32),
        "norm_gain": jnp.clip(1.0 + 0.18 * jax.random.normal(key_list[3], (KV_RANK,), jnp.float32), 0.1, 1.9),
        "w_kv_up": normal_values(key_list[4], (KV_RANK, HEADS * (PLAIN_PART_SIZE + VHEAD)), KV_RANK ** -0.5, 0.25, ((1, 16),)),
        "w_out": normal_values(key_list[5], (HEADS * VHEAD, D), (HEADS * VHEAD) ** -0.5, 0.046875, ((0, 16), (1, 8))),
    }


def position_of(block_order, row_total, block_len):
    row_index = jnp.arange(row_total, dtype=jnp.int32)
    return block_order[row_index // block_len] * block_len + row_index % block_len

def normalize(latents, norm_gain):
    compressed = latents[:, :KV_RANK].astype(jnp.float32)
    mean_square = lax.optimization_barrier(jnp.mean(compressed * compressed, axis=-1, keepdims=True))
    return (compressed * lax.rsqrt(mean_square + 1e-06) * norm_gain.astype(jnp.float32)).astype(jnp.bfloat16)

def reference(queries, latents, block_order, norm_gain, w_kv_up, w_out):
    highest = lax.Precision.HIGHEST
    positions = position_of(block_order, TOKENS, BLOCK)
    normed = normalize(latents, norm_gain)
    normed_wide = normed.astype(jnp.float32)
    rope_keys = latents[:, KV_RANK:].astype(jnp.float32)
    visible = positions[None, :] <= positions[:, None]
    score_scale = 1.0 / (PLAIN_PART_SIZE + ROPE) ** 0.5
    group_size = 8
    group_count = HEADS // group_size
    query_groups = queries.reshape(TOKENS, group_count, group_size, PLAIN_PART_SIZE + ROPE).transpose(1, 0, 2, 3)
    weight_groups = w_kv_up.reshape(KV_RANK, group_count, group_size, PLAIN_PART_SIZE + VHEAD).transpose(1, 0, 2, 3)

    def one_group(paired):
        query_part, weight_part = paired
        weight_wide = weight_part.astype(jnp.float32)
        keys_nope = jnp.einsum('tr,rhd->thd', normed_wide, weight_wide[..., :PLAIN_PART_SIZE], precision=highest).astype(jnp.bfloat16)
        values = jnp.einsum('tr,rhd->thd', normed_wide, weight_wide[..., PLAIN_PART_SIZE:], precision=highest).astype(jnp.bfloat16)
        keys_nope, values = lax.optimization_barrier((keys_nope, values))
        keys_nope = keys_nope.astype(jnp.float32)
        values = values.astype(jnp.float32)
        query_wide = query_part.astype(jnp.float32)
        logits = jnp.einsum('qhd,thd->qht', query_wide[..., :PLAIN_PART_SIZE], keys_nope, precision=highest)
        logits = logits + jnp.einsum('qhd,td->qht', query_wide[..., PLAIN_PART_SIZE:], rope_keys, precision=highest)
        logits = jnp.where(visible[:, None, :], logits * score_scale, -jnp.inf)
        peak = lax.optimization_barrier(jnp.max(logits, axis=-1, keepdims=True))
        expo = jnp.exp(logits - peak)
        probs = (expo / lax.optimization_barrier(jnp.sum(expo, axis=-1, keepdims=True))).astype(jnp.bfloat16)
        context = jnp.einsum('qht,thd->qhd', probs.astype(jnp.float32), values, precision=highest)
        return context.astype(jnp.bfloat16)
    contexts = lax.map(one_group, (query_groups, weight_groups))
    context = contexts.transpose(1, 0, 2, 3).reshape(TOKENS, HEADS * VHEAD)
    return jnp.dot(context, w_out, preferred_element_type=jnp.float32).astype(jnp.bfloat16)
```

```python
import functools

import jax
import jax.numpy as jnp
from jax import lax
from jax.experimental import pallas as pl
from jax.experimental.pallas import tpu as pltpu
from jax.sharding import Mesh, PartitionSpec as P

KV_RANK = 512
ROPE = 64
NOPE = 128
VHEAD = 128
BLOCK = 256
NX, NZ, NY = 4, 2, 4
TOKENS = 4096
PIECE = 128
TILE = 512
SCALE = (NOPE + ROPE) ** -0.5 * 1.4426950408889634
F32, BF16 = jnp.float32, jnp.bfloat16
NT = (((1,), (1,)), ((), ()))


def shift(a, axis, size, step):
    return lax.ppermute(a, axis, [(i, (i + step) % size) for i in range(size)])


def kv_kernel(place, *refs):
    pieces, w_ref, g_ref, k_ref, v_ref = refs[:8], refs[8], refs[9], refs[10], refs[11]
    s = pl.program_id(0)
    lane = lax.broadcasted_iota(jnp.int32, (PIECE // 2, 128), 1)
    gain = g_ref[...]
    wide = []
    for ref in pieces:
        x = jnp.concatenate([ref[0, 128 * i : 128 * (i + 1), :] for i in range(4)], axis=1).astype(F32)
        ms = jnp.mean(x * x, axis=-1, keepdims=True)
        wide.append((x * lax.rsqrt(ms + 1e-06) * gain).astype(BF16))
    normed = jnp.concatenate(wide, axis=0)
    out = jnp.dot(normed, w_ref[...], preferred_element_type=F32)
    for n, ref in enumerate(pieces):
        at = pl.multiple_of(place[s * 8 + n] * PIECE, PIECE)
        rope = ref[0, 512:576, :].astype(F32)
        turned = pltpu.roll(rope, 64, 1)
        low = jnp.concatenate([rope, turned], axis=0)
        high = jnp.concatenate([turned, rope], axis=0)
        lanes = jnp.concatenate([lane, lane], axis=0)
        o = out[PIECE * n : PIECE * (n + 1)]
        k0 = jnp.concatenate([o[:, 0:128], jnp.where(lanes < 64, low, 0.0)], axis=1)
        k1 = jnp.concatenate([o[:, 256:384], o[:, 384:512] + jnp.where(lanes >= 64, high, 0.0)], axis=1)
        k_ref[0, pl.ds(at, PIECE), :] = (k0 * SCALE).astype(BF16)
        k_ref[1, pl.ds(at, PIECE), :] = (k1 * SCALE).astype(BF16)
        v_ref[pl.ds(at, PIECE), :] = o[:, 512:768].astype(BF16)


def keys_values(place, pieces, weights, gain):
    rows = pl.BlockSpec((1, 576, 128), lambda s, place: (s, 0, 0))
    whole = lambda *shape: pl.BlockSpec(shape, lambda s, place: (0,) * len(shape))
    return pl.pallas_call(
        kv_kernel,
        out_shape=(
            jax.ShapeDtypeStruct((2, TOKENS, 256), BF16),
            jax.ShapeDtypeStruct((TOKENS, 256), BF16),
        ),
        grid_spec=pltpu.PrefetchScalarGridSpec(
            num_scalar_prefetch=1,
            grid=(NX,),
            in_specs=[rows] * 8 + [whole(KV_RANK, 768), whole(1, KV_RANK)],
            out_specs=(whole(2, TOKENS, 256), whole(TOKENS, 256)),
        ),
        compiler_params=pltpu.CompilerParams(vmem_limit_bytes=50 * 2**20),
        cost_estimate=pl.CostEstimate(flops=6 * 10**9, bytes_accessed=12 * 10**6, transcendentals=4096),
        name="keys_values",
    )(place, *pieces, weights, gain)


def attend_kernel(info, q_ref, k_ref, v_ref, o_ref, acc, peak, total):
    for b in range(2):
        pos = info[1 + b]
        q_rows = pl.ds(b * BLOCK, BLOCK)
        q = (q_ref[0, q_rows, 0:256], q_ref[0, q_rows, 128:384])
        full = pos // (TILE // BLOCK)

        def tile(at, first):
            for h in range(2):
                s = lax.dot_general(q[h], k_ref[h, pl.ds(at, TILE), :], NT, preferred_element_type=F32)
                if first:
                    row = pos * BLOCK + lax.broadcasted_iota(jnp.int32, (BLOCK, TILE), 0)
                    col = at + lax.broadcasted_iota(jnp.int32, (BLOCK, TILE), 1)
                    s = jnp.where(col <= row, s, -jnp.inf)
                top = jnp.max(s, axis=-1, keepdims=True)
                if not first:
                    old = peak[h]
                    top = jnp.maximum(old, top)
                    keep = jnp.exp2(old - top)
                p = jnp.exp2(s - top)
                part = p[:, 0:128]
                for i in range(1, TILE // 128):
                    part = part + p[:, 128 * i : 128 * (i + 1)]
                pv = jnp.dot(p.astype(BF16), v_ref[pl.ds(at, TILE), 128 * h : 128 * (h + 1)], preferred_element_type=F32)
                if first:
                    total[h] = part
                    acc[h] = pv
                else:
                    total[h] = total[h] * keep + part
                    acc[h] = acc[h] * keep + pv
                peak[h] = jnp.broadcast_to(top, (BLOCK, 1))

        tile(pl.multiple_of(full * TILE, TILE), True)

        @pl.loop(0, full)
        def _(i):
            tile(pl.multiple_of(i * TILE, TILE), False)

        for h in range(2):
            norm = jnp.sum(total[h], axis=-1, keepdims=True)
            o_ref[q_rows, 128 * h : 128 * (h + 1)] = (acc[h] / norm).astype(BF16)


def attend(info, q, k, v):
    return pl.pallas_call(
        attend_kernel,
        out_shape=jax.ShapeDtypeStruct((2 * BLOCK, 256), BF16),
        grid_spec=pltpu.PrefetchScalarGridSpec(
            num_scalar_prefetch=1,
            grid=(1,),
            in_specs=[
                pl.BlockSpec((1, 512, 384), lambda i, info: (info[0], 0, 0)),
                pl.BlockSpec((2, TOKENS, 256), lambda i, info: (0, 0, 0)),
                pl.BlockSpec((TOKENS, 256), lambda i, info: (0, 0)),
            ],
            out_specs=pl.BlockSpec((2 * BLOCK, 256), lambda i, info: (0, 0)),
            scratch_shapes=[
                pltpu.VMEM((2, BLOCK, 128), F32),
                pltpu.VMEM((2, BLOCK, 1), F32),
                pltpu.VMEM((2, BLOCK, 128), F32),
            ],
        ),
        compiler_params=pltpu.CompilerParams(vmem_limit_bytes=50 * 2**20),
        cost_estimate=pl.CostEstimate(flops=6 * 10**9, bytes_accessed=7 * 10**6, transcendentals=2 * 10**6),
        name="attend",
    )(info, q, k, v)


def on_device(queries, latents, block_order, norm_gain, w_kv_up, w_out):
    x, zl, zh = lax.axis_index("x"), lax.axis_index("zl"), lax.axis_index("zh")
    y, c = lax.axis_index("y"), lax.axis_index("c")
    rel = jnp.arange(4, dtype=jnp.int32)

    mine = lax.dynamic_slice_in_dim(latents, y * PIECE, PIECE, 0)
    rope = mine[:, KV_RANK:]
    packed = jnp.concatenate(
        [mine[:, 128 * i : 128 * (i + 1)] for i in range(4)]
        + [jnp.concatenate([rope[:64], rope[64:]], axis=1)],
        axis=0,
    )

    def across(s):
        pairs = []
        for xs in range(NX):
            for zs in range(2):
                for cs in range(2):
                    pairs.append(((xs * 2 + zs) * 2 + cs, (((xs + s) % NX) * 2 + cs) * 2 + zs))
        return lax.ppermute(packed, ("x", "zl", "c"), pairs)

    plane = jnp.stack([across(s) for s in range(NX)])
    own = [plane] + [shift(plane, "y", NY, t) for t in range(1, NY)]
    other = [shift(a, "c", 2, 1) for a in own]

    blocks = queries.reshape(512, NX, 384)

    def heads_of(s):
        return lax.dynamic_index_in_dim(blocks, (x + s) % NX, 1, keepdims=False)

    q = jnp.stack([heads_of(0)] + [shift(heads_of(s), "x", NX, s) for s in range(1, NX)])

    far = shift(w_out, "zl", 2, 1)
    w_cols = jnp.concatenate([jnp.where(zl == 0, w_out, far), jnp.where(zl == 0, far, w_out)], axis=1)
    w_rel = jnp.concatenate(
        [lax.dynamic_slice_in_dim(w_cols, ((x - s) % NX) * 256, 256, 0) for s in range(NX)], axis=0
    )
    up = lax.dynamic_slice_in_dim(w_kv_up, x * 512, 512, 1)
    z64 = jnp.zeros((KV_RANK, 64), BF16)
    up = jnp.concatenate(
        [up[:, 0:128], z64, z64, z64, up[:, 256:384], z64, up[:, 128:256], up[:, 384:512]], axis=1
    )

    xs = (x - rel)[:, None, None] % NX
    zs = jnp.stack([c, 1 - c])[None, :, None]
    ys = (y - rel)[None, None, :] % NY
    slot = 2 * (2 * xs + zs) + ys // 2
    place = (block_order[slot] * 2 + ys % 2).reshape(-1).astype(jnp.int32)
    k, v = keys_values(place, own + other, up, norm_gain.reshape(1, KV_RANK))

    done = []
    for j in range(NX):
        first = 2 * (2 * j + zl)
        info = jnp.stack([(x - j) % NX, block_order[first], block_order[first + 1]]).astype(jnp.int32)
        ctx = attend(info, q, k, v)
        ctx = jnp.concatenate([ctx] + [shift(ctx, "x", NX, s) for s in range(1, NX)], axis=1)
        part = jnp.dot(ctx, w_rel, preferred_element_type=F32).astype(BF16)
        part = part.reshape(2, NY, 2, 32, 1792)
        keep = lax.dynamic_index_in_dim(part, c, 2, keepdims=False)
        give = lax.dynamic_index_in_dim(part, 1 - c, 2, keepdims=False)
        pair = (keep.astype(F32) + shift(give, "c", 2, 1).astype(F32)).astype(BF16)
        total = lax.dynamic_index_in_dim(pair, y, 1, keepdims=False).astype(F32)
        for s in range(1, NY):
            give = lax.dynamic_index_in_dim(pair, (y + s) % NY, 1, keepdims=False)
            total = total + shift(give, "y", NY, s).astype(F32)
        total = total.astype(BF16)
        give = lax.dynamic_index_in_dim(total, 1 - zh, 0, keepdims=False)
        keep = lax.dynamic_index_in_dim(total, zh, 0, keepdims=False)
        done.append((keep.astype(F32) + shift(give, "zh", 2, 1).astype(F32)).astype(BF16))
    out = lax.all_to_all(jnp.stack(done), "x", 0, 0, tiled=True)
    return out.transpose(1, 0, 2).reshape(32, NX * 1792)


def solution(mesh):
    fine = Mesh(mesh.devices.reshape(NX, NZ, 2, NY, 2), ("x", "zl", "zh", "y", "c"))
    ctx, head = ("x", "zl"), ("zh", "y", "c")
    in_specs = (P(ctx, head), P(ctx, None), P(), P(), P(None, head), P(head, ctx))
    return jax.shard_map(
        on_device, mesh=fine, in_specs=in_specs, out_specs=P(ctx + head, None), check_vma=False
    )
```

```python
import functools

import jax
import jax.numpy as jnp
from jax import lax
from jax.experimental import pallas as pl
from jax.experimental.pallas import tpu as pltpu
from jax.sharding import Mesh, PartitionSpec as P

KV_RANK = 512
ROPE = 64
NOPE = 128
BLOCK = 256
NX, NZ, NY = 4, 2, 4
TOKENS = 4096
PIECE = 128
COLS = 1792
TILE = 512
SCALE = (NOPE + ROPE) ** -0.5 * 1.4426950408889634
F32, BF16 = jnp.float32, jnp.bfloat16
NT = (((1,), (1,)), ((), ()))
VMEM = pl.BlockSpec(memory_space=pltpu.VMEM)
SMEM = pl.BlockSpec(memory_space=pltpu.SMEM)


def shift(a, axis, size, step):
    return lax.ppermute(a, axis, [(i, (i + step) % size) for i in range(size)])


def params(mib):
    return pltpu.CompilerParams(vmem_limit_bytes=mib * 2**20)


def cost(flops, nbytes):
    return pl.CostEstimate(flops=flops, bytes_accessed=nbytes, transcendentals=0)


def kv_kernel(turns, info, order, *refs):
    groups, (w_ref, g_ref) = refs[:4], refs[4:6]
    k_ref, v_ref = refs[-2:]
    x, y, c = info[0], info[2], info[3]
    zeros = jnp.zeros((64, PIECE), BF16)
    for n, ref in enumerate(groups):
        zs = c if n < len(turns) else 1 - c
        ys = lax.rem(y + turns[n % len(turns)], NY)
        wide = []
        for s in range(NX):
            a = ref[s, 0:KV_RANK, :].astype(F32)
            ms = jnp.sum(a * a, axis=0, keepdims=True) * (1.0 / KV_RANK)
            wide.append((a * lax.rsqrt(ms + 1e-06) * g_ref[...]).astype(BF16))
        out = jnp.dot(w_ref[...], jnp.concatenate(wide, axis=1), preferred_element_type=F32)
        for s in range(NX):
            xs = lax.rem(x - s + NX, NX)
            row = order[2 * (2 * xs + zs) + ys // 2] * BLOCK + lax.rem(ys, 2) * PIECE
            at = pl.ds(pl.multiple_of(row, PIECE), PIECE)
            o = out[:, PIECE * s : PIECE * (s + 1)]
            rope = (ref[s, KV_RANK : KV_RANK + ROPE, :].astype(F32) * SCALE).astype(BF16)
            k0 = (o[0:128] * SCALE).astype(BF16)
            k1 = (o[256:384] * SCALE).astype(BF16)
            k_ref[0, :, at] = jnp.concatenate([k0, rope, zeros], axis=0)
            k_ref[1, :, at] = jnp.concatenate([zeros, k1, rope], axis=0)
            v_ref[0, :, at] = o[128:256].astype(BF16)
            v_ref[1, :, at] = o[384:512].astype(BF16)


def keys_values(turns, info, order, groups, weights, gain, before=()):
    ins = 2 + len(groups) + 2
    return pl.pallas_call(
        functools.partial(kv_kernel, turns),
        out_shape=(
            jax.ShapeDtypeStruct((2, 256, TOKENS), BF16),
            jax.ShapeDtypeStruct((2, 128, TOKENS), BF16),
        ),
        in_specs=[SMEM, SMEM] + [VMEM] * (len(groups) + 2 + len(before)),
        out_specs=(VMEM, VMEM),
        input_output_aliases={ins + n: n for n in range(len(before))},
        compiler_params=params(20),
        cost_estimate=cost(3 * 10**9, 5 * 10**6),
        name=f"keys_values_{len(before) // 2}",
    )(info, order, *groups, weights, gain, *before)


def attend_kernel(j, info, order, q0, q1, q2, q3, k_ref, v_ref, keep_ref, give_ref, q_ref, s_ref, peak, total, acc):
    for n in range(2):
        turn = lax.rem(info[0] - (j + n) + NX, NX)
        for s, ref in enumerate((q0, q1, q2, q3)):
            @pl.when(turn == s)
            def _():
                q_ref[512 * n : 512 * (n + 1)] = ref[...]

    @pl.loop(0, 2)
    def _(n):
        pos = [order[2 * (2 * (j + n) + info[1]) + r] for r in range(2)]
        full = [a * BLOCK // TILE for a in pos]

        def logits(i, r, slot):
            at = pl.multiple_of(i * TILE, TILE)
            rows = pl.ds(pl.multiple_of(2 * n * BLOCK, BLOCK) + r * BLOCK, BLOCK)
            for h in range(2):
                q = q_ref[rows, 128 * h : 128 * h + 256]
                s_ref[r, slot, h] = jnp.dot(q, k_ref[h, :, pl.ds(at, TILE)], preferred_element_type=F32)

        def weigh(i, r, slot, masked):
            at = pl.multiple_of(i * TILE, TILE)
            for h in range(2):
                s = s_ref[r, slot, h]
                if masked:
                    ahead = lax.broadcasted_iota(jnp.int32, s.shape, 1) - lax.broadcasted_iota(jnp.int32, s.shape, 0)
                    s = jnp.where(ahead <= pos[r] * BLOCK - at, s, -jnp.inf)
                cols = [s[:, 128 * c : 128 * (c + 1)] for c in range(TILE // 128)]
                top = jnp.max(functools.reduce(jnp.maximum, cols), axis=-1, keepdims=True)
                old = peak[r, h]
                top = jnp.maximum(old, jnp.broadcast_to(top, (BLOCK, 128)))
                keep = jnp.exp2(old - top)
                ps = [jnp.exp2(col - top) for col in cols]
                p = jnp.concatenate([a.astype(BF16) for a in ps], axis=1)
                pv = lax.dot_general(p, v_ref[h, :, pl.ds(at, TILE)], NT, preferred_element_type=F32)
                peak[r, h] = top
                total[r, h] = total[r, h] * keep + functools.reduce(jnp.add, ps)
                acc[r, h] = acc[r, h] * keep + pv

        def two_tiles(i, blocks):
            for r in blocks:
                logits(2 * i + 1, r, 1)
            for r in blocks:
                weigh(2 * i, r, 0, False)
            for r in blocks:
                logits(2 * i + 2, r, 0)
            for r in blocks:
                weigh(2 * i + 1, r, 1, False)

        peak[...] = jnp.full(peak.shape, -1e30, F32)
        total[...] = jnp.zeros(total.shape, F32)
        acc[...] = jnp.zeros(acc.shape, F32)
        for r in range(2):
            logits(0, r, 0)
        shared = jnp.minimum(full[0], full[1]) // 2

        @pl.loop(0, shared)
        def _(i):
            two_tiles(i, (0, 1))

        for r in range(2):

            @pl.loop(shared, full[r] // 2)
            def _(i):
                two_tiles(i, (r,))

            @pl.when(lax.rem(full[r], 2) == 1)
            def _():
                logits(full[r], r, 1)
                weigh(full[r] - 1, r, 0, False)

        for r in range(2):
            weigh(full[r], r, lax.rem(full[r], 2), True)
        for r in range(2):
            for h in range(2):
                norm = jnp.sum(total[r, h], axis=-1, keepdims=True)
                o = (acc[r, h] / norm).astype(BF16)
                for y in range(NY):
                    even, odd = o[64 * y : 64 * y + 32], o[64 * y + 32 : 64 * y + 64]
                    at = pl.multiple_of(128 * y + 64 * n + 32 * r, 32)
                    to = (pl.ds(at, 32), slice(128 * h, 128 * h + 128))
                    keep_ref[to] = jnp.where(info[3] == 0, even, odd)
                    give_ref[to] = jnp.where(info[3] == 0, odd, even)


def attend(j, info, order, qs, k, v):
    half = jax.ShapeDtypeStruct((2 * BLOCK, 256), BF16)
    return pl.pallas_call(
        functools.partial(attend_kernel, j),
        out_shape=(half, half),
        in_specs=[SMEM, SMEM] + [VMEM] * 6,
        out_specs=(VMEM, VMEM),
        scratch_shapes=[pltpu.VMEM((4 * BLOCK, 384), BF16), pltpu.VMEM((2, 2, 2, BLOCK, TILE), F32)]
        + [pltpu.VMEM((2, 2, BLOCK, 128), F32)] * 3,
        compiler_params=params(20),
        cost_estimate=cost(10**10, 7 * 10**6),
        name=f"attend_{j}",
    )(info, order, *qs, k, v)


def project_kernel(split, info, *refs):
    outs = refs[-3:] if split else refs[-1:]
    refs = refs[: -len(outs)]
    ctx, (w_ref, w_far) = refs[:-2], refs[-2:]
    if len(ctx) == 1:
        pieces, starts = [ctx[0][n] for n in range(NX)], [256 * n for n in range(NX)]
    else:
        pieces = [ref[...] for ref in ctx]
        starts = [pl.multiple_of(lax.rem(info[0] - s + NX, NX) * 256, 256) for s in range(NX)]
    left = jnp.concatenate(pieces, axis=1)
    right = jnp.concatenate([ref[pl.ds(at, 256), :] for at in starts for ref in (w_ref, w_far)], axis=0)
    out = jnp.dot(left, right, preferred_element_type=F32).astype(BF16)

    def by_y(ref):
        for y in range(NY):
            ref[y] = out[128 * y : 128 * (y + 1)]

    if not split:
        by_y(outs[0])
        return

    @pl.when(pl.program_id(0) == 0)
    def _():
        by_y(outs[0])

    @pl.when(pl.program_id(0) == 1)
    def _():
        for y in range(NY):
            for n in range(2):
                at, rows = 128 * y + 64 * n, slice(32 * n, 32 * (n + 1))
                low, high = out[at : at + 32], out[at + 32 : at + 64]
                outs[1][y, rows] = jnp.where(info[4] == 0, low, high)
                outs[2][y, rows] = jnp.where(info[4] == 0, high, low)


def project(j, info, ctx, w, w_far, split):
    width = COLS // 2
    whole = [pl.BlockSpec(a.shape, lambda n, rank=a.ndim: (0,) * rank) for a in ctx]
    column = pl.BlockSpec((1024, width), lambda n: (0, n))
    if split:
        shapes = [(NY, 128, width), (NY, 64, width), (NY, 64, width)]
        out_specs = [pl.BlockSpec(a, lambda n, rank=len(a): (0,) * rank) for a in shapes]
    else:
        shapes = [(NY, 128, COLS)]
        out_specs = [pl.BlockSpec((NY, 128, width), lambda n: (0, 0, n))]
    return pl.pallas_call(
        functools.partial(project_kernel, split),
        out_shape=[jax.ShapeDtypeStruct(a, BF16) for a in shapes],
        grid=(2,),
        in_specs=[SMEM] + whole + [column, column],
        out_specs=out_specs,
        compiler_params=params(56),
        cost_estimate=cost(4 * 10**9, 7 * 10**6),
        name=f"project_{j}",
    )(info, *ctx, w, w_far)


def hold(*values):
    return lax.optimization_barrier(values)


def on_device(queries, latents, block_order, norm_gain, w_kv_up, w_out):
    x, zl, zh = lax.axis_index("x"), lax.axis_index("zl"), lax.axis_index("zh")
    y, c = lax.axis_index("y"), lax.axis_index("c")
    info = jnp.stack([x, zl, y, c, zh]).astype(jnp.int32)
    w = lax.all_gather(w_out, "zl", axis=1, tiled=True)

    columns = latents.T

    def across(part, s):
        pairs = []
        for xs in range(NX):
            for zs in range(2):
                for cs in range(2):
                    pairs.append(((xs * 2 + zs) * 2 + cs, (((xs + s) % NX) * 2 + cs) * 2 + zs))
        return lax.ppermute(part, ("x", "zl", "c"), pairs)

    near = lax.dynamic_slice_in_dim(columns, y * PIECE, PIECE, 1)
    opposite = lax.dynamic_slice_in_dim(columns, (y + 2) % NY * PIECE, PIECE, 1)
    both = jnp.stack([near, opposite])
    landed = [across(both, s) for s in range(NX)]
    near = jnp.stack([a[0] for a in landed])
    opposite = jnp.stack([a[1] for a in landed])

    qs = [lax.dynamic_slice_in_dim(queries, (x + s) % NX * 384, 384, 1) for s in range(NX)]
    up = lax.dynamic_slice_in_dim(w_kv_up, x * 512, 512, 1).T
    gain = jnp.broadcast_to(norm_gain[:, None], (KV_RANK, PIECE))
    near, opposite, qs, up, gain = hold(near, opposite, qs, up, gain)
    before, after = shift(near, "y", NY, 1), shift(near, "y", NY, 3)
    qs = [qs[0]] + [shift(qs[s], "x", NX, s) for s in range(1, NX)]
    near_far, opposite_far = shift(near, "c", 2, 1), shift(opposite, "c", 2, 1)
    kv = keys_values((0, 2), info, block_order, (near, opposite, near_far, opposite_far), up, gain)
    before, after, info1, *others = hold(before, after, info, *qs[1:])
    qs = [qs[0]] + others
    before_far, after_far = shift(before, "c", 2, 1), shift(after, "c", 2, 1)
    k, v = keys_values((3, 1), info1, block_order, (before, after, before_far, after_far), up, gain, kv)

    def attention(j, info):
        keep, give = attend(j, info, block_order, qs, k, v)
        return jnp.concatenate([keep, shift(give, "c", 2, 1)], axis=1)

    def add_up(a):
        return jnp.sum(a.astype(F32), axis=0).astype(BF16)

    a0, info2, w = hold(attention(0, info1), info1, w)
    w_far = shift(w, "c", 2, 1)
    g0, a1 = [a0] + [shift(a0, "x", NX, s) for s in (1, 2, 3)], attention(2, info2)
    g0, a1, info3, w_far = hold(g0, a1, info2, w_far)
    g1 = lax.all_gather(a1, "x", axis=0, tiled=False)

    def over_y(a):
        return add_up(lax.all_to_all(a, "y", 0, 0, tiled=True))

    def over_z(keep, give):
        return (keep.astype(F32) + shift(give, "zh", 2, 1).astype(F32)).astype(BF16)

    def halves(a):
        a = a.reshape(2, 2, 32, a.shape[-1])
        pick = lambda n: lax.dynamic_index_in_dim(a, n, 1, keepdims=False)
        return pick(zh), pick(1 - zh)

    (p0,) = project(0, info3, g0, w, w_far, False)
    y0 = lax.all_to_all(p0, "y", 0, 0, tiled=True)
    p0, g1, info4 = hold(p0, g1, info3)
    left, keep, give, y0 = hold(*project(1, info4, [g1], w, w_far, True), y0)
    left, right = over_y(left), over_z(keep, give)
    left, right = over_z(*halves(left)), over_y(right).reshape(2, 32, COLS // 2)
    s0 = over_z(*halves(add_up(y0)))
    total = jnp.concatenate([s0, jnp.concatenate([left, right], axis=2)])
    out = lax.all_to_all(total, "x", 0, 0, tiled=True)
    return out.transpose(1, 0, 2).reshape(32, NX * COLS)


def solution(mesh):
    fine = Mesh(mesh.devices.reshape(NX, NZ, 2, NY, 2), ("x", "zl", "zh", "y", "c"))
    ctx, head = ("x", "zl"), ("zh", "y", "c")
    in_specs = (P(ctx, head), P(ctx, None), P(), P(), P(None, head), P(head, ctx))
    return jax.shard_map(
        on_device, mesh=fine, in_specs=in_specs, out_specs=P(ctx + head, None), check_vma=False
    )
```

```python
import functools

import jax
import jax.numpy as jnp
from jax import lax
from jax.experimental import pallas as pl
from jax.experimental.pallas import tpu as pltpu
from jax.sharding import Mesh, PartitionSpec as P

KV_RANK = 512
ROPE = 64
NOPE = 128
BLOCK = 256
NX, NZ, NY = 4, 2, 4
TOKENS = 4096
PIECE = 128
COLS = 1792
TILE = 512
SCALE = (NOPE + ROPE) ** -0.5 * 1.4426950408889634
F32, BF16 = jnp.float32, jnp.bfloat16
NT = (((1,), (1,)), ((), ()))
VMEM = pl.BlockSpec(memory_space=pltpu.VMEM)
SMEM = pl.BlockSpec(memory_space=pltpu.SMEM)


def shift(a, axis, size, step):
    return lax.ppermute(a, axis, [(i, (i + step) % size) for i in range(size)])


def params(mib):
    return pltpu.CompilerParams(vmem_limit_bytes=mib * 2**20)


def cost(flops, nbytes):
    return pl.CostEstimate(flops=flops, bytes_accessed=nbytes, transcendentals=0)


def kv_kernel(turns, info, order, *refs):
    groups, (w_ref, g_ref) = refs[:4], refs[4:6]
    k_ref, v_ref = refs[-2:]
    x, y, c = info[0], info[2], info[3]
    zeros = jnp.zeros((64, PIECE), BF16)
    for n, ref in enumerate(groups):
        zs = c if n < len(turns) else 1 - c
        ys = lax.rem(y + turns[n % len(turns)], NY)
        wide = []
        for s in range(NX):
            a = ref[s, 0:KV_RANK, :].astype(F32)
            ms = jnp.sum(a * a, axis=0, keepdims=True) * (1.0 / KV_RANK)
            wide.append((a * lax.rsqrt(ms + 1e-06) * g_ref[...]).astype(BF16))
        out = jnp.dot(w_ref[...], jnp.concatenate(wide, axis=1), preferred_element_type=F32)
        for s in range(NX):
            xs = lax.rem(x - s + NX, NX)
            row = order[2 * (2 * xs + zs) + ys // 2] * BLOCK + lax.rem(ys, 2) * PIECE
            at = pl.ds(pl.multiple_of(row, PIECE), PIECE)
            o = out[:, PIECE * s : PIECE * (s + 1)]
            rope = (ref[s, KV_RANK : KV_RANK + ROPE, :].astype(F32) * SCALE).astype(BF16)
            k0 = (o[0:128] * SCALE).astype(BF16)
            k1 = (o[256:384] * SCALE).astype(BF16)
            k_ref[0, :, at] = jnp.concatenate([k0, rope, zeros], axis=0)
            k_ref[1, :, at] = jnp.concatenate([zeros, k1, rope], axis=0)
            v_ref[0, :, at] = o[128:256].astype(BF16)
            v_ref[1, :, at] = o[384:512].astype(BF16)


def keys_values(turns, info, order, groups, weights, gain, before=()):
    ins = 2 + len(groups) + 2
    return pl.pallas_call(
        functools.partial(kv_kernel, turns),
        out_shape=(
            jax.ShapeDtypeStruct((2, 256, TOKENS), BF16),
            jax.ShapeDtypeStruct((2, 128, TOKENS), BF16),
        ),
        in_specs=[SMEM, SMEM] + [VMEM] * (len(groups) + 2 + len(before)),
        out_specs=(VMEM, VMEM),
        input_output_aliases={ins + n: n for n in range(len(before))},
        compiler_params=params(20),
        cost_estimate=cost(3 * 10**9, 5 * 10**6),
        name=f"keys_values_{len(before) // 2}",
    )(info, order, *groups, weights, gain, *before)


def attend_kernel(j, info, order, q0, q1, q2, q3, k_ref, v_ref, keep_ref, give_ref, q_ref, s_ref, peak, total, acc):
    for n in range(2):
        turn = lax.rem(info[0] - (j + n) + NX, NX)
        for s, ref in enumerate((q0, q1, q2, q3)):
            @pl.when(turn == s)
            def _():
                q_ref[512 * n : 512 * (n + 1)] = ref[...]

    @pl.loop(0, 2)
    def _(n):
        pos = [order[2 * (2 * (j + n) + info[1]) + r] for r in range(2)]
        full = [a * BLOCK // TILE for a in pos]

        def logits(i, r, slot):
            at = pl.multiple_of(i * TILE, TILE)
            rows = pl.ds(pl.multiple_of(2 * n * BLOCK, BLOCK) + r * BLOCK, BLOCK)
            for h in range(2):
                q = q_ref[rows, 128 * h : 128 * h + 256]
                s_ref[r, slot, h] = jnp.dot(q, k_ref[h, :, pl.ds(at, TILE)], preferred_element_type=F32)

        def weigh(i, r, slot, masked):
            at = pl.multiple_of(i * TILE, TILE)
            for h in range(2):
                s = s_ref[r, slot, h]
                if masked:
                    ahead = lax.broadcasted_iota(jnp.int32, s.shape, 1) - lax.broadcasted_iota(jnp.int32, s.shape, 0)
                    s = jnp.where(ahead <= pos[r] * BLOCK - at, s, -jnp.inf)
                cols = [s[:, 128 * c : 128 * (c + 1)] for c in range(TILE // 128)]
                top = jnp.max(functools.reduce(jnp.maximum, cols), axis=-1, keepdims=True)
                old = peak[r, h]
                top = jnp.maximum(old, jnp.broadcast_to(top, (BLOCK, 128)))
                keep = jnp.exp2(old - top)
                ps = [jnp.exp2(col - top) for col in cols]
                p = jnp.concatenate([a.astype(BF16) for a in ps], axis=1)
                pv = lax.dot_general(p, v_ref[h, :, pl.ds(at, TILE)], NT, preferred_element_type=F32)
                peak[r, h] = top
                total[r, h] = total[r, h] * keep + functools.reduce(jnp.add, ps)
                acc[r, h] = acc[r, h] * keep + pv

        def two_tiles(i, blocks):
            for r in blocks:
                logits(2 * i + 1, r, 1)
            for r in blocks:
                weigh(2 * i, r, 0, False)
            for r in blocks:
                logits(2 * i + 2, r, 0)
            for r in blocks:
                weigh(2 * i + 1, r, 1, False)

        peak[...] = jnp.full(peak.shape, -1e30, F32)
        total[...] = jnp.zeros(total.shape, F32)
        acc[...] = jnp.zeros(acc.shape, F32)
        for r in range(2):
            logits(0, r, 0)
        shared = jnp.minimum(full[0], full[1]) // 2

        @pl.loop(0, shared)
        def _(i):
            two_tiles(i, (0, 1))

        for r in range(2):

            @pl.loop(shared, full[r] // 2)
            def _(i):
                two_tiles(i, (r,))

            @pl.when(lax.rem(full[r], 2) == 1)
            def _():
                logits(full[r], r, 1)
                weigh(full[r] - 1, r, 0, False)

        for r in range(2):
            weigh(full[r], r, lax.rem(full[r], 2), True)
        for r in range(2):
            for h in range(2):
                norm = jnp.sum(total[r, h], axis=-1, keepdims=True)
                o = (acc[r, h] / norm).astype(BF16)
                for y in range(NY):
                    even, odd = o[64 * y : 64 * y + 32], o[64 * y + 32 : 64 * y + 64]
                    at = pl.multiple_of(128 * y + 64 * n + 32 * r, 32)
                    to = (pl.ds(at, 32), slice(128 * h, 128 * h + 128))
                    keep_ref[to] = jnp.where(info[3] == 0, even, odd)
                    give_ref[to] = jnp.where(info[3] == 0, odd, even)


def attend(j, info, order, qs, k, v):
    half = jax.ShapeDtypeStruct((2 * BLOCK, 256), BF16)
    return pl.pallas_call(
        functools.partial(attend_kernel, j),
        out_shape=(half, half),
        in_specs=[SMEM, SMEM] + [VMEM] * 6,
        out_specs=(VMEM, VMEM),
        scratch_shapes=[pltpu.VMEM((4 * BLOCK, 384), BF16), pltpu.VMEM((2, 2, 2, BLOCK, TILE), F32)]
        + [pltpu.VMEM((2, 2, BLOCK, 128), F32)] * 3,
        compiler_params=params(20),
        cost_estimate=cost(10**10, 7 * 10**6),
        name=f"attend_{j}",
    )(info, order, *qs, k, v)


def project_kernel(split, info, *refs):
    outs = refs[-3:] if split else refs[-1:]
    refs = refs[: -len(outs)]
    ctx, (w_ref, w_far) = refs[:-2], refs[-2:]
    if len(ctx) == 1:
        pieces, starts = [ctx[0][n] for n in range(NX)], [256 * n for n in range(NX)]
    else:
        pieces = [ref[...] for ref in ctx]
        starts = [pl.multiple_of(lax.rem(info[0] - s + NX, NX) * 256, 256) for s in range(NX)]
    left = jnp.concatenate(pieces, axis=1)
    right = jnp.concatenate([ref[pl.ds(at, 256), :] for at in starts for ref in (w_ref, w_far)], axis=0)
    out = jnp.dot(left, right, preferred_element_type=F32).astype(BF16)

    def by_y(ref):
        for y in range(NY):
            ref[y] = out[128 * y : 128 * (y + 1)]

    if not split:
        by_y(outs[0])
        return

    @pl.when(pl.program_id(0) == 0)
    def _():
        by_y(outs[0])

    @pl.when(pl.program_id(0) == 1)
    def _():
        for y in range(NY):
            for n in range(2):
                at, rows = 128 * y + 64 * n, slice(32 * n, 32 * (n + 1))
                low, high = out[at : at + 32], out[at + 32 : at + 64]
                outs[1][y, rows] = jnp.where(info[4] == 0, low, high)
                outs[2][y, rows] = jnp.where(info[4] == 0, high, low)


def project(j, info, ctx, w, w_far, split):
    width = COLS // 2
    whole = [pl.BlockSpec(a.shape, lambda n, rank=a.ndim: (0,) * rank) for a in ctx]
    column = pl.BlockSpec((1024, width), lambda n: (0, n))
    if split:
        shapes = [(NY, 128, width), (NY, 64, width), (NY, 64, width)]
        out_specs = [pl.BlockSpec(a, lambda n, rank=len(a): (0,) * rank) for a in shapes]
    else:
        shapes = [(NY, 128, COLS)]
        out_specs = [pl.BlockSpec((NY, 128, width), lambda n: (0, 0, n))]
    return pl.pallas_call(
        functools.partial(project_kernel, split),
        out_shape=[jax.ShapeDtypeStruct(a, BF16) for a in shapes],
        grid=(2,),
        in_specs=[SMEM] + whole + [column, column],
        out_specs=out_specs,
        compiler_params=params(56),
        cost_estimate=cost(4 * 10**9 if split else 4 * 10**10, 7 * 10**6),
        name=f"project_{j}",
    )(info, *ctx, w, w_far)


def hold(*values):
    return lax.optimization_barrier(values)


def on_device(queries, latents, block_order, norm_gain, w_kv_up, w_out):
    x, zl, zh = lax.axis_index("x"), lax.axis_index("zl"), lax.axis_index("zh")
    y, c = lax.axis_index("y"), lax.axis_index("c")
    info = jnp.stack([x, zl, y, c, zh]).astype(jnp.int32)
    w = lax.all_gather(w_out, "zl", axis=1, tiled=True)

    columns = latents.T

    def across(part, s):
        pairs = []
        for xs in range(NX):
            for zs in range(2):
                for cs in range(2):
                    pairs.append(((xs * 2 + zs) * 2 + cs, (((xs + s) % NX) * 2 + cs) * 2 + zs))
        return lax.ppermute(part, ("x", "zl", "c"), pairs)

    near = lax.dynamic_slice_in_dim(columns, y * PIECE, PIECE, 1)
    opposite = lax.dynamic_slice_in_dim(columns, (y + 2) % NY * PIECE, PIECE, 1)
    both = jnp.stack([near, opposite])
    landed = [across(both, s) for s in range(NX)]
    near = jnp.stack([a[0] for a in landed])
    opposite = jnp.stack([a[1] for a in landed])

    qs = [lax.dynamic_slice_in_dim(queries, (x + s) % NX * 384, 384, 1) for s in range(NX)]
    up = lax.dynamic_slice_in_dim(w_kv_up, x * 512, 512, 1).T
    gain = jnp.broadcast_to(norm_gain[:, None], (KV_RANK, PIECE))
    near, opposite, qs, up, gain = hold(near, opposite, qs, up, gain)
    before, after = shift(near, "y", NY, 1), shift(near, "y", NY, 3)
    qs = [qs[0]] + [shift(qs[s], "x", NX, s) for s in range(1, NX)]
    near_far, opposite_far = shift(near, "c", 2, 1), shift(opposite, "c", 2, 1)
    kv = keys_values((0, 2), info, block_order, (near, opposite, near_far, opposite_far), up, gain)
    before, after, info1, *others = hold(before, after, info, *qs[1:])
    qs = [qs[0]] + others
    before_far, after_far = shift(before, "c", 2, 1), shift(after, "c", 2, 1)
    k, v = keys_values((3, 1), info1, block_order, (before, after, before_far, after_far), up, gain, kv)

    def attention(j, info):
        keep, give = attend(j, info, block_order, qs, k, v)
        return jnp.concatenate([keep, shift(give, "c", 2, 1)], axis=1)

    def add_up(a):
        return jnp.sum(a.astype(F32), axis=0).astype(BF16)

    a0, info2, w = hold(attention(0, info1), info1, w)
    w_far = shift(w, "c", 2, 1)
    g0, a1 = [a0] + [shift(a0, "x", NX, s) for s in (1, 2, 3)], attention(2, info2)
    g1 = lax.all_gather(a1, "x", axis=0, tiled=False)
    g0, a1, info3, w_far = hold(g0, a1, info2, w_far)

    def over_y(a):
        return add_up(lax.all_to_all(a, "y", 0, 0, tiled=True))

    def over_z(keep, give):
        return (keep.astype(F32) + shift(give, "zh", 2, 1).astype(F32)).astype(BF16)

    def halves(a):
        a = a.reshape(2, 2, 32, a.shape[-1])
        pick = lambda n: lax.dynamic_index_in_dim(a, n, 1, keepdims=False)
        return pick(zh), pick(1 - zh)

    (p0,) = project(0, info3, g0, w, w_far, False)
    y0 = lax.all_to_all(p0, "y", 0, 0, tiled=True)
    p0, g1, info4 = hold(p0, g1, info3)
    left, keep, give, y0 = hold(*project(1, info4, [g1], w, w_far, True), y0)
    left, right = over_y(left), over_z(keep, give)
    left, right = over_z(*halves(left)), over_y(right).reshape(2, 32, COLS // 2)
    s0 = over_z(*halves(add_up(y0)))
    total = jnp.concatenate([s0, jnp.concatenate([left, right], axis=2)])
    out = lax.all_to_all(total, "x", 0, 0, tiled=True)
    return out.transpose(1, 0, 2).reshape(32, NX * COLS)


def solution(mesh):
    fine = Mesh(mesh.devices.reshape(NX, NZ, 2, NY, 2), ("x", "zl", "zh", "y", "c"))
    ctx, head = ("x", "zl"), ("zh", "y", "c")
    in_specs = (P(ctx, head), P(ctx, None), P(), P(), P(None, head), P(head, ctx))
    return jax.shard_map(
        on_device, mesh=fine, in_specs=in_specs, out_specs=P(ctx + head, None), check_vma=False
    )
```

```python
import functools

import jax
import jax.numpy as jnp
from jax import lax
from jax.experimental import pallas as pl
from jax.experimental.pallas import tpu as pltpu
from jax.sharding import Mesh, PartitionSpec as P

KV_RANK = 512
ROPE = 64
NOPE = 128
BLOCK = 256
NX, NZ, NY = 4, 2, 4
TOKENS = 4096
PIECE = 128
COLS = 1792
TILE = 512
SCALE = (NOPE + ROPE) ** -0.5 * 1.4426950408889634
F32, BF16 = jnp.float32, jnp.bfloat16
NT = (((1,), (1,)), ((), ()))
VMEM = pl.BlockSpec(memory_space=pltpu.VMEM)
SMEM = pl.BlockSpec(memory_space=pltpu.SMEM)
ANY = pl.BlockSpec(memory_space=pl.ANY)


def shift(a, axis, size, step):
    return lax.ppermute(a, axis, [(i, (i + step) % size) for i in range(size)])


def params(mib):
    return pltpu.CompilerParams(vmem_limit_bytes=mib * 2**20)


def cost(flops, nbytes):
    return pl.CostEstimate(flops=flops, bytes_accessed=nbytes, transcendentals=0)


def kv_kernel(turns, info, order, *refs):
    groups, (w_ref, g_ref) = refs[:4], refs[4:6]
    k_ref, v_ref = refs[-2:]
    x, y, c = info[0], info[2], info[3]
    zeros = jnp.zeros((64, PIECE), BF16)
    for n, ref in enumerate(groups):
        zs = c if n < len(turns) else 1 - c
        ys = lax.rem(y + turns[n % len(turns)], NY)
        wide = []
        for s in range(NX):
            a = ref[s, 0:KV_RANK, :].astype(F32)
            ms = jnp.sum(a * a, axis=0, keepdims=True) * (1.0 / KV_RANK)
            wide.append((a * lax.rsqrt(ms + 1e-06) * g_ref[...]).astype(BF16))
        out = jnp.dot(w_ref[...], jnp.concatenate(wide, axis=1), preferred_element_type=F32)
        for s in range(NX):
            xs = lax.rem(x - s + NX, NX)
            row = order[2 * (2 * xs + zs) + ys // 2] * BLOCK + lax.rem(ys, 2) * PIECE
            at = pl.ds(pl.multiple_of(row, PIECE), PIECE)
            o = out[:, PIECE * s : PIECE * (s + 1)]
            rope = (ref[s, KV_RANK : KV_RANK + ROPE, :].astype(F32) * SCALE).astype(BF16)
            k0 = (o[0:128] * SCALE).astype(BF16)
            k1 = (o[256:384] * SCALE).astype(BF16)
            k_ref[0, :, at] = jnp.concatenate([k0, rope, zeros], axis=0)
            k_ref[1, :, at] = jnp.concatenate([zeros, k1, rope], axis=0)
            v_ref[0, :, at] = o[128:256].astype(BF16)
            v_ref[1, :, at] = o[384:512].astype(BF16)


def keys_values(turns, info, order, groups, weights, gain, before=()):
    ins = 2 + len(groups) + 2
    return pl.pallas_call(
        functools.partial(kv_kernel, turns),
        out_shape=(
            jax.ShapeDtypeStruct((2, 256, TOKENS), BF16),
            jax.ShapeDtypeStruct((2, 128, TOKENS), BF16),
        ),
        in_specs=[SMEM, SMEM] + [VMEM] * (len(groups) + 2 + len(before)),
        out_specs=(VMEM, VMEM),
        input_output_aliases={ins + n: n for n in range(len(before))},
        compiler_params=params(20),
        cost_estimate=cost(3 * 10**9, 5 * 10**6),
        name=f"keys_values_{len(before) // 2}",
    )(info, order, *groups, weights, gain, *before)


def attend_kernel(j, info, order, q0, q1, q2, q3, k_ref, v_ref, keep_ref, give_ref, q_ref, s_ref, peak, total, acc):
    for n in range(2):
        turn = lax.rem(info[0] - (j + n) + NX, NX)
        for s, ref in enumerate((q0, q1, q2, q3)):
            @pl.when(turn == s)
            def _():
                q_ref[512 * n : 512 * (n + 1)] = ref[...]

    @pl.loop(0, 2)
    def _(n):
        pos = [order[2 * (2 * (j + n) + info[1]) + r] for r in range(2)]
        full = [a * BLOCK // TILE for a in pos]

        def logits(i, r, slot):
            at = pl.multiple_of(i * TILE, TILE)
            rows = pl.ds(pl.multiple_of(2 * n * BLOCK, BLOCK) + r * BLOCK, BLOCK)
            for h in range(2):
                q = q_ref[rows, 128 * h : 128 * h + 256]
                s_ref[r, slot, h] = jnp.dot(q, k_ref[h, :, pl.ds(at, TILE)], preferred_element_type=F32)

        def weigh(i, r, slot, masked):
            at = pl.multiple_of(i * TILE, TILE)
            for h in range(2):
                s = s_ref[r, slot, h]
                if masked:
                    ahead = lax.broadcasted_iota(jnp.int32, s.shape, 1) - lax.broadcasted_iota(jnp.int32, s.shape, 0)
                    s = jnp.where(ahead <= pos[r] * BLOCK - at, s, -jnp.inf)
                cols = [s[:, 128 * c : 128 * (c + 1)] for c in range(TILE // 128)]
                top = jnp.max(functools.reduce(jnp.maximum, cols), axis=-1, keepdims=True)
                old = peak[r, h]
                top = jnp.maximum(old, jnp.broadcast_to(top, (BLOCK, 128)))
                keep = jnp.exp2(old - top)
                ps = [jnp.exp2(col - top) for col in cols]
                p = jnp.concatenate([a.astype(BF16) for a in ps], axis=1)
                pv = lax.dot_general(p, v_ref[h, :, pl.ds(at, TILE)], NT, preferred_element_type=F32)
                peak[r, h] = top
                total[r, h] = total[r, h] * keep + functools.reduce(jnp.add, ps)
                acc[r, h] = acc[r, h] * keep + pv

        def two_tiles(i, blocks):
            for r in blocks:
                logits(2 * i + 1, r, 1)
            for r in blocks:
                weigh(2 * i, r, 0, False)
            for r in blocks:
                logits(2 * i + 2, r, 0)
            for r in blocks:
                weigh(2 * i + 1, r, 1, False)

        peak[...] = jnp.full(peak.shape, -1e30, F32)
        total[...] = jnp.zeros(total.shape, F32)
        acc[...] = jnp.zeros(acc.shape, F32)
        for r in range(2):
            logits(0, r, 0)
        shared = jnp.minimum(full[0], full[1]) // 2

        @pl.loop(0, shared)
        def _(i):
            two_tiles(i, (0, 1))

        for r in range(2):

            @pl.loop(shared, full[r] // 2)
            def _(i):
                two_tiles(i, (r,))

            @pl.when(lax.rem(full[r], 2) == 1)
            def _():
                logits(full[r], r, 1)
                weigh(full[r] - 1, r, 0, False)

        for r in range(2):
            weigh(full[r], r, lax.rem(full[r], 2), True)
        for r in range(2):
            for h in range(2):
                norm = jnp.sum(total[r, h], axis=-1, keepdims=True)
                o = (acc[r, h] / norm).astype(BF16)
                for y in range(NY):
                    even, odd = o[64 * y : 64 * y + 32], o[64 * y + 32 : 64 * y + 64]
                    at = pl.multiple_of(128 * y + 64 * n + 32 * r, 32)
                    to = (pl.ds(at, 32), slice(128 * h, 128 * h + 128))
                    keep_ref[to] = jnp.where(info[3] == 0, even, odd)
                    give_ref[to] = jnp.where(info[3] == 0, odd, even)


def attend(j, info, order, qs, k, v):
    half = jax.ShapeDtypeStruct((2 * BLOCK, 256), BF16)
    return pl.pallas_call(
        functools.partial(attend_kernel, j),
        out_shape=(half, half),
        in_specs=[SMEM, SMEM] + [VMEM] * 6,
        out_specs=(VMEM, VMEM),
        scratch_shapes=[pltpu.VMEM((4 * BLOCK, 384), BF16), pltpu.VMEM((2, 2, 2, BLOCK, TILE), F32)]
        + [pltpu.VMEM((2, 2, BLOCK, 128), F32)] * 3,
        compiler_params=params(20),
        cost_estimate=cost(10**10, 7 * 10**6),
        name=f"attend_{j}",
    )(info, order, *qs, k, v)


def project_kernel(info, c0, c1, c2, c3, w_ref, w_far, out_ref):
    starts = [pl.multiple_of(lax.rem(info[0] - s + NX, NX) * 256, 256) for s in range(NX)]
    left = jnp.concatenate([ref[...] for ref in (c0, c1, c2, c3)], axis=1)
    right = jnp.concatenate([ref[0, pl.ds(at, 256), :] for at in starts for ref in (w_ref, w_far)], axis=0)
    out = jnp.dot(left, right, preferred_element_type=F32).astype(BF16)
    for y in range(NY):
        out_ref[y] = out[128 * y : 128 * (y + 1)]


def project(info, ctx, w, w_far):
    width = COLS // 2
    whole = pl.BlockSpec((512, 512), lambda n: (0, 0))
    column = pl.BlockSpec((1, 1024, width), lambda n: (n, 0, 0))
    return pl.pallas_call(
        project_kernel,
        out_shape=jax.ShapeDtypeStruct((NY, 128, COLS), BF16),
        grid=(2,),
        in_specs=[SMEM] + [whole] * NX + [column, column],
        out_specs=pl.BlockSpec((NY, 128, width), lambda n: (0, 0, n)),
        compiler_params=params(56),
        cost_estimate=cost(4 * 10**10, 7 * 10**6),
        name="project_0",
    )(info, *ctx, w, w_far)


def fetch_kernel(tie, w_hbm, far_hbm, w_ref, far_ref, done_ref, sems):
    del tie
    done_ref[...] = jnp.zeros(done_ref.shape, F32)
    copies = [pltpu.make_async_copy(w_hbm, w_ref, sems.at[0]), pltpu.make_async_copy(far_hbm, far_ref, sems.at[1])]
    for copy in copies:
        copy.start()
    for copy in copies:
        copy.wait()


def fetch(tie, w, w_far):
    return pl.pallas_call(
        fetch_kernel,
        out_shape=[jax.ShapeDtypeStruct(w.shape, BF16)] * 2 + [jax.ShapeDtypeStruct((8, 128), F32)],
        in_specs=[SMEM, ANY, ANY],
        out_specs=[VMEM] * 3,
        scratch_shapes=[pltpu.SemaphoreType.DMA((2,))],
        compiler_params=params(16),
        cost_estimate=cost(4 * 10**9, 7 * 10**6),
        name="fetch_weights",
    )(tie, w, w_far)


def project_split_kernel(info, ctx, w_ref, w_far, left_ref, keep_ref, give_ref):
    left = jnp.concatenate([ctx[n] for n in range(NX)], axis=1)
    for n in range(2):
        right = jnp.concatenate(
            [ref[n, 256 * i : 256 * (i + 1), :] for i in range(NX) for ref in (w_ref, w_far)], axis=0
        )
        out = jnp.dot(left, right, preferred_element_type=F32).astype(BF16)
        for y in range(NY):
            if n == 0:
                left_ref[y] = out[128 * y : 128 * (y + 1)]
                continue
            for i in range(2):
                at, rows = 128 * y + 64 * i, slice(32 * i, 32 * (i + 1))
                low, high = out[at : at + 32], out[at + 32 : at + 64]
                keep_ref[y, rows] = jnp.where(info[4] == 0, low, high)
                give_ref[y, rows] = jnp.where(info[4] == 0, high, low)


def project_split(info, ctx, w, w_far):
    width = COLS // 2
    shapes = [(NY, 128, width), (NY, 64, width), (NY, 64, width)]
    return pl.pallas_call(
        project_split_kernel,
        out_shape=[jax.ShapeDtypeStruct(a, BF16) for a in shapes],
        in_specs=[SMEM] + [VMEM] * 3,
        out_specs=[VMEM] * 3,
        compiler_params=params(20),
        cost_estimate=cost(4 * 10**9, 7 * 10**6),
        name="project_1",
    )(info, ctx, w, w_far)


def hold(*values):
    return lax.optimization_barrier(values)


def on_device(queries, latents, block_order, norm_gain, w_kv_up, w_out):
    x, zl, zh = lax.axis_index("x"), lax.axis_index("zl"), lax.axis_index("zh")
    y, c = lax.axis_index("y"), lax.axis_index("c")
    info = jnp.stack([x, zl, y, c, zh]).astype(jnp.int32)
    w = lax.all_gather(w_out, "zl", axis=0, tiled=False)

    columns = latents.T

    def across(part, s):
        pairs = []
        for xs in range(NX):
            for zs in range(2):
                for cs in range(2):
                    pairs.append(((xs * 2 + zs) * 2 + cs, (((xs + s) % NX) * 2 + cs) * 2 + zs))
        return lax.ppermute(part, ("x", "zl", "c"), pairs)

    near = lax.dynamic_slice_in_dim(columns, y * PIECE, PIECE, 1)
    opposite = lax.dynamic_slice_in_dim(columns, (y + 2) % NY * PIECE, PIECE, 1)
    both = jnp.stack([near, opposite])
    landed = [across(both, s) for s in range(NX)]
    near = jnp.stack([a[0] for a in landed])
    opposite = jnp.stack([a[1] for a in landed])

    qs = [lax.dynamic_slice_in_dim(queries, (x + s) % NX * 384, 384, 1) for s in range(NX)]
    up = lax.dynamic_slice_in_dim(w_kv_up, x * 512, 512, 1).T
    gain = jnp.broadcast_to(norm_gain[:, None], (KV_RANK, PIECE))
    near, opposite, qs, up, gain = hold(near, opposite, qs, up, gain)
    before, after = shift(near, "y", NY, 1), shift(near, "y", NY, 3)
    qs = [qs[0]] + [shift(qs[s], "x", NX, s) for s in range(1, NX)]
    near_far, opposite_far = shift(near, "c", 2, 1), shift(opposite, "c", 2, 1)
    kv = keys_values((0, 2), info, block_order, (near, opposite, near_far, opposite_far), up, gain)
    before, after, info1, *others = hold(before, after, info, *qs[1:])
    qs = [qs[0]] + others
    before_far, after_far = shift(before, "c", 2, 1), shift(after, "c", 2, 1)
    k, v = keys_values((3, 1), info1, block_order, (before, after, before_far, after_far), up, gain, kv)

    def attention(j, info):
        keep, give = attend(j, info, block_order, qs, k, v)
        return jnp.concatenate([keep, shift(give, "c", 2, 1)], axis=1)

    def add_up(a):
        return jnp.sum(a.astype(F32), axis=0).astype(BF16)

    a0, info2, w = hold(attention(0, info1), info1, w)
    w_far = shift(w, "c", 2, 1)
    g0, a1 = [a0] + [shift(a0, "x", NX, s) for s in (1, 2, 3)], attention(2, info2)
    g1 = lax.all_gather(a1, "x", axis=0, tiled=False)
    g0, a1, info3, w_far = hold(g0, a1, info2, w_far)

    def over_y(a):
        return add_up(lax.all_to_all(a, "y", 0, 0, tiled=True))

    def over_z(keep, give):
        return (keep.astype(F32) + shift(give, "zh", 2, 1).astype(F32)).astype(BF16)

    def halves(a):
        a = a.reshape(2, 2, 32, a.shape[-1])
        pick = lambda n: lax.dynamic_index_in_dim(a, n, 1, keepdims=False)
        return pick(zh), pick(1 - zh)

    p0 = project(info3, g0, w, w_far)
    y0 = lax.all_to_all(p0, "y", 0, 0, tiled=True)
    p0, info5 = hold(p0, info3)
    w, w_far, done = fetch(info5, w, w_far)
    g1, info4 = hold(g1, info5 + done[0, : info.size].astype(jnp.int32))
    left, keep, give, y0 = hold(*project_split(info4, g1, w, w_far), y0)
    left, right = over_y(left), over_z(keep, give)
    left, right = over_z(*halves(left)), over_y(right).reshape(2, 32, COLS // 2)
    s0 = over_z(*halves(add_up(y0)))
    total = jnp.concatenate([s0, jnp.concatenate([left, right], axis=2)])
    out = lax.all_to_all(total, "x", 0, 0, tiled=True)
    return out.transpose(1, 0, 2).reshape(32, NX * COLS)


def solution(mesh):
    fine = Mesh(mesh.devices.reshape(NX, NZ, 2, NY, 2), ("x", "zl", "zh", "y", "c"))
    ctx, head = ("x", "zl"), ("zh", "y", "c")
    in_specs = (P(ctx, head), P(ctx, None), P(), P(), P(None, head), P(head, ctx))
    return jax.shard_map(
        on_device, mesh=fine, in_specs=in_specs, out_specs=P(ctx + head, None), check_vma=False
    )
```
